32 devices in a mesh: vocab: 2 (over core), sample: 4 (over y, x), prompt: 4 (over z).
Axes of the slice: x: 2, y: 2, z: 4, core: 2. Of those that a mesh axis runs over, the one named last changes fastest.
Arguments:
- hidden: bfloat16 [1024, 4608], P(('sample', 'prompt'), 'vocab'), may hold values from -12 to 12
- gain: float32 [4608], replicated, may hold values from 0.25 to 1.75
- head: bfloat16 [4608, 64000], P(None, ('vocab', 'sample', 'prompt')), may hold values from -0.25 to 0.25
- candidates: int32 [32, 16], replicated, may hold values from 0 to 63999
- row_prompt: int32 [1024], replicated, may hold values from 0 to 31, as said below
Outputs:
- log_votes: float32 [32, 16], replicated
- row_lse: float32 [1024], P(('sample', 'prompt'))
The draws below stay inside these ranges and needn't reach their ends.
Inputs may be any that keep to these rules, and one draw needn't show every extreme that they name: `row_prompt`: every prompt has at least one row; the rows of a prompt may stand anywhere among the 1024 rows.
All inputs are finite; a program needn't handle non-finite values.
Results may differ from the reference program's by a relative error of at most 0.00051.
Values may be sent and summed in bfloat16 or wider, within the bound.
A program may use at most 128 MiB of HBM per device.

```python
import jax
import jax.numpy as jnp
from jax import lax

D = 4608
V_DEV = 2000
CANDS = 16
VOCAB = 64000
ROWS = 1024
PROMPTS = 32


def draw_row_prompt(key, part):
    first, second = jax.random.split(jax.random.fold_in(key, 7))
    base = jax.random.randint(first, (ROWS,), 0, PROMPTS)
    order = jax.random.permutation(second, PROMPTS)
    places = jnp.arange(ROWS)
    return jnp.where(places < PROMPTS, order[jnp.minimum(places, PROMPTS - 1)], base).astype(jnp.int32)


def place_ends(array, key, least, top_value):
    dims = array.shape
    spot = [jax.random.randint(jax.random.fold_in(key, axis), (), 0, dims[axis]) for axis in range(len(dims))]
    array = array.at[tuple(spot)].set(least)
    longest = dims.index(max(dims))
    spot[longest] = (spot[longest] + 1) % dims[longest]
    return array.at[tuple(spot)].set(top_value)


def shard_levels(own_key, shape, cuts, low, top_value):
    def one(dim, parts):
        steps = jax.random.uniform(jax.random.fold_in(jax.random.fold_in(own_key, 6), dim), (parts,), jnp.float32, low / len(cuts), top_value / len(cuts))
        return jnp.repeat(jnp.exp(steps), shape[dim] // parts).reshape((-1,) + (1,) * (len(shape) - dim - 1))

    factor_of = one(*cuts[0])
    for cut in cuts[1:]:
        factor_of = factor_of * one(*cut)
    return factor_of


def bell_draw(own_key, dims, spread, reach, pieces=(), held_as=jnp.bfloat16):
    entries = spread * jax.random.normal(own_key, dims, jnp.float32)
    if pieces:
        entries = entries * shard_levels(own_key, dims, pieces, -0.22, 0.18)
    return jnp.clip(entries, -reach, reach).astype(held_as)


def setup_inputs(seed: int = 0) -> dict:
    splits = jax.random.split(jax.random.key(seed), 6)
    hidden = bell_draw(splits[0], (ROWS, D), 2.0, 12.0, ((0, 16), (1, 2)))
    gain = jnp.clip(1.0 + 0.15 * jax.random.normal(splits[1], (D,), jnp.float32), 0.25, 1.75)
    head = bell_draw(splits[2], (D, VOCAB), (D // 9) ** -0.5, 0.25, ((1, 32),))
    candidates = place_ends(jax.random.randint(splits[3], (PROMPTS, CANDS), 0, VOCAB), jax.random.fold_in(splits[3], 1), 0, VOCAB - 1).astype(jnp.int32)
    row_prompt = draw_row_prompt(jax.random.fold_in(splits[5], 71), 0)
    return {"hidden": hidden, "gain": gain, "head": head, "candidates": candidates, "row_prompt": row_prompt}


CAP = 30.0
EPS = 1e-06

def reference(hidden, gain, head, candidates, row_prompt):
    xf = hidden.astype(jnp.float32)
    mean_sq = lax.optimization_barrier(jnp.mean(xf * xf, axis=1, keepdims=True))
    normed = (xf * lax.rsqrt(mean_sq + EPS) * gain).astype(jnp.bfloat16)
    onehot = (row_prompt[:, None] == jnp.arange(PROMPTS, dtype=jnp.int32)[None, :]).astype(jnp.float32)
    wanted = candidates[row_prompt]
    blocks = VOCAB // V_DEV

    def step(index, carry):
        total, numer = carry
        begin = (index * V_DEV).astype(jnp.int32)
        columns = lax.dynamic_slice_in_dim(head, begin, V_DEV, 1)
        logits = CAP * jnp.tanh(jnp.dot(normed, columns, preferred_element_type=jnp.float32) / CAP)
        exps = jnp.exp(logits)
        local = wanted - begin
        inside = (local >= 0) & (local < V_DEV)
        picked = jnp.take_along_axis(exps, jnp.clip(local, 0, V_DEV - 1), axis=1)
        return (total + lax.optimization_barrier(jnp.sum(exps, axis=1)), numer + jnp.where(inside, picked, jnp.zeros_like(picked)))
    start = (jnp.zeros((ROWS,), jnp.float32), jnp.zeros((ROWS, CANDS), jnp.float32))
    total, numer = lax.fori_loop(0, blocks, step, start)
    prob = numer / total[:, None]
    tally = jnp.dot(onehot.T, prob, precision=lax.Precision.HIGHEST, preferred_element_type=jnp.float32)
    return (jnp.log(tally), jnp.log(total))
```

```python
import functools

import jax
import jax.numpy as jnp
from jax import lax
from jax.experimental import pallas as pl
from jax.experimental.pallas import tpu as pltpu
from jax.sharding import PartitionSpec as P

CAP = 30.0
EPS = 1e-06
AXES = ("vocab", "sample", "prompt")
MESH = pl.DeviceIdType.MESH


def place(flat, sizes):
    return (flat // (sizes[1] * sizes[2]), flat // sizes[2] % sizes[1], flat % sizes[2])


def finish_kernel(
    sizes, sums_ref, terms_ref, tally_ref, totals_ref,
    sums_in, part, part_in, send_a, recv_a, send_b, recv_b,
):
    devices = sizes[0] * sizes[1] * sizes[2]
    me = lax.axis_index(AXES)
    barrier = pltpu.get_barrier_semaphore()

    def greet(step, carry):
        peer = (me + step) % devices
        pl.semaphore_signal(barrier, inc=1, device_id=place(peer, sizes), device_id_type=MESH)
        return carry

    lax.fori_loop(1, devices, greet, 0)
    pl.semaphore_wait(barrier, devices - 1)

    def push(source, target, send_sem, recv_sem):
        def out(step, carry):
            peer = (me + step) % devices
            pltpu.make_async_remote_copy(
                src_ref=source,
                dst_ref=target.at[me],
                send_sem=send_sem.at[step],
                recv_sem=recv_sem.at[me],
                device_id=place(peer, sizes),
                device_id_type=MESH,
            ).start()
            return carry

        lax.fori_loop(1, devices, out, 0)

    def collect(source, target, send_sem, recv_sem):
        def arrive(step, carry):
            peer = (me + step) % devices
            pltpu.make_async_remote_copy(
                src_ref=source,
                dst_ref=target.at[peer],
                send_sem=send_sem.at[step],
                recv_sem=recv_sem.at[peer],
                device_id=place(peer, sizes),
                device_id_type=MESH,
            ).wait()
            return carry

        lax.fori_loop(1, devices, arrive, 0)

    push(sums_ref, sums_in, send_a, recv_a)
    sums_in[me] = sums_ref[...]
    collect(sums_ref, sums_in, send_a, recv_a)
    total = jnp.sum(sums_in[...], axis=0)
    totals_ref[...] = total
    part[...] = jnp.dot(
        1.0 / total, terms_ref[...],
        precision=lax.Precision.HIGHEST, preferred_element_type=jnp.float32,
    )
    push(part, part_in, send_b, recv_b)
    part_in[me] = part[...]
    collect(part, part_in, send_b, recv_b)
    tally_ref[...] = jnp.log(jnp.sum(part_in[...], axis=0))


def finish(sums, terms):
    sizes = tuple(lax.axis_size(axis) for axis in AXES)
    devices = sizes[0] * sizes[1] * sizes[2]
    rows, picks = terms.shape
    vmem = pl.BlockSpec(memory_space=pltpu.VMEM)
    return pl.pallas_call(
        functools.partial(finish_kernel, sizes),
        out_shape=(
            jax.ShapeDtypeStruct((1, picks), jnp.float32),
            jax.ShapeDtypeStruct((1, rows), jnp.float32),
        ),
        in_specs=[vmem] * 2,
        out_specs=(vmem, vmem),
        scratch_shapes=[
            pltpu.VMEM((devices, 1, rows), jnp.float32),
            pltpu.VMEM((1, picks), jnp.float32),
            pltpu.VMEM((devices, 1, picks), jnp.float32),
            pltpu.SemaphoreType.DMA((devices,)),
            pltpu.SemaphoreType.DMA((devices,)),
            pltpu.SemaphoreType.DMA((devices,)),
            pltpu.SemaphoreType.DMA((devices,)),
        ],
        compiler_params=pltpu.CompilerParams(
            collective_id=1, has_side_effects=True, vmem_limit_bytes=24 << 20
        ),
    )(sums, terms)


def plain_head(hidden, gain, head, wanted, row_prompt, cands):
    width = head.shape[0]
    vocab_dev = head.shape[1]
    shards = lax.axis_size("vocab")
    row_dev = hidden.shape[0]
    cols = hidden.shape[1]
    xf = hidden.astype(jnp.float32)
    squared = lax.psum(jnp.sum(xf * xf, axis=1), "vocab")
    scale = lax.rsqrt(squared / width + EPS)
    gain_part = lax.dynamic_slice_in_dim(gain, lax.axis_index("vocab") * cols, cols)
    normed = (xf * scale[:, None] * gain_part[None, :]).astype(jnp.bfloat16)
    pieces = lax.all_gather(normed[None], AXES, axis=0, tiled=True)
    groups = pieces.shape[0] // shards
    pieces = pieces.reshape(shards, groups, row_dev, cols)
    weight = head.reshape(shards, cols, vocab_dev)
    raw = jnp.einsum("vgrd,vdc->grc", pieces, weight, preferred_element_type=jnp.float32)
    exps = jnp.exp(CAP * jnp.tanh(raw.reshape(groups * row_dev, vocab_dev) / CAP))
    sums = jnp.sum(exps, axis=1)
    columns = jnp.arange(vocab_dev, dtype=jnp.int32)
    selector = (columns[:, None] == wanted[None, :]).astype(jnp.bfloat16)
    high = lax.reduce_precision(exps, 8, 7)
    low = (exps - high).astype(jnp.bfloat16)
    high = high.astype(jnp.bfloat16)
    picked = jnp.dot(high, selector, preferred_element_type=jnp.float32)
    picked = picked + jnp.dot(low, selector, preferred_element_type=jnp.float32)
    prompt_of = jnp.arange(wanted.shape[0], dtype=jnp.int32) // cands
    terms = jnp.where(row_prompt[:, None] == prompt_of[None, :], picked, 0.0)
    return sums[None, :], terms


def body(hidden, gain, head, candidates, row_prompt):
    row_dev = hidden.shape[0]
    prompts, cands = candidates.shape
    offset = lax.axis_index(AXES) * head.shape[1]
    wanted = candidates.reshape(prompts * cands) - offset
    sums, terms = plain_head(hidden, gain, head, wanted, row_prompt, cands)
    votes, totals = finish(sums, terms)
    group = lax.axis_index(("sample", "prompt"))
    row_lse = lax.dynamic_slice_in_dim(jnp.log(totals[0]), group * row_dev, row_dev, 0)
    return votes.reshape(prompts, cands), row_lse


def solution(mesh):
    placed = (
        P(("sample", "prompt"), "vocab"),
        P(),
        P(None, AXES),
        P(),
        P(),
    )
    return jax.shard_map(
        body, mesh=mesh, in_specs=placed, out_specs=(P(), P(("sample", "prompt"))), check_vma=False
    )
```

```python
import functools

import jax
import jax.numpy as jnp
from jax import lax
from jax.experimental import pallas as pl
from jax.experimental.pallas import tpu as pltpu
from jax.sharding import PartitionSpec as P

CAP = 30.0
EPS = 1e-06
AXES = ("vocab", "sample", "prompt")
MESH = pl.DeviceIdType.MESH


def place(flat, sizes):
    return (flat // (sizes[1] * sizes[2]), flat // sizes[2] % sizes[1], flat % sizes[2])


def finish_kernel(
    sizes, sums_ref, terms_ref, tally_ref, totals_ref,
    sums_in, part, part_in, send_a, recv_a, send_b, recv_b,
):
    devices = sizes[0] * sizes[1] * sizes[2]
    me = lax.axis_index(AXES)
    barrier = pltpu.get_barrier_semaphore()

    def greet(step, carry):
        peer = (me + step) % devices
        pl.semaphore_signal(barrier, inc=1, device_id=place(peer, sizes), device_id_type=MESH)
        return carry

    lax.fori_loop(1, devices, greet, 0)
    pl.semaphore_wait(barrier, devices - 1)

    def push(source, target, send_sem, recv_sem):
        def out(step, carry):
            peer = (me + step) % devices
            pltpu.make_async_remote_copy(
                src_ref=source,
                dst_ref=target.at[me],
                send_sem=send_sem.at[step],
                recv_sem=recv_sem.at[me],
                device_id=place(peer, sizes),
                device_id_type=MESH,
            ).start()
            return carry

        lax.fori_loop(1, devices, out, 0)

    def collect(source, target, send_sem, recv_sem):
        def arrive(step, carry):
            peer = (me + step) % devices
            pltpu.make_async_remote_copy(
                src_ref=source,
                dst_ref=target.at[peer],
                send_sem=send_sem.at[step],
                recv_sem=recv_sem.at[peer],
                device_id=place(peer, sizes),
                device_id_type=MESH,
            ).wait()
            return carry

        lax.fori_loop(1, devices, arrive, 0)

    push(sums_ref, sums_in, send_a, recv_a)
    sums_in[me] = sums_ref[...]
    collect(sums_ref, sums_in, send_a, recv_a)
    total = jnp.sum(sums_in[...], axis=0)
    totals_ref[...] = total
    part[...] = jnp.dot(
        1.0 / total, terms_ref[...],
        precision=lax.Precision.HIGHEST, preferred_element_type=jnp.float32,
    )
    push(part, part_in, send_b, recv_b)
    part_in[me] = part[...]
    collect(part, part_in, send_b, recv_b)
    tally_ref[...] = jnp.log(jnp.sum(part_in[...], axis=0))


def finish(sums, terms):
    sizes = tuple(lax.axis_size(axis) for axis in AXES)
    devices = sizes[0] * sizes[1] * sizes[2]
    rows, picks = terms.shape
    vmem = pl.BlockSpec(memory_space=pltpu.VMEM)
    return pl.pallas_call(
        functools.partial(finish_kernel, sizes),
        out_shape=(
            jax.ShapeDtypeStruct((1, picks), jnp.float32),
            jax.ShapeDtypeStruct((1, rows), jnp.float32),
        ),
        in_specs=[vmem] * 2,
        out_specs=(vmem, vmem),
        scratch_shapes=[
            pltpu.VMEM((devices, 1, rows), jnp.float32),
            pltpu.VMEM((1, picks), jnp.float32),
            pltpu.VMEM((devices, 1, picks), jnp.float32),
            pltpu.SemaphoreType.DMA((devices,)),
            pltpu.SemaphoreType.DMA((devices,)),
            pltpu.SemaphoreType.DMA((devices,)),
            pltpu.SemaphoreType.DMA((devices,)),
        ],
        compiler_params=pltpu.CompilerParams(
            collective_id=1, has_side_effects=True, vmem_limit_bytes=24 << 20
        ),
    )(sums, terms)


def plain_head(hidden, gain, head, wanted, row_prompt, cands):
    width = head.shape[0]
    vocab_dev = head.shape[1]
    shards = lax.axis_size("vocab")
    row_dev = hidden.shape[0]
    cols = hidden.shape[1]
    xf = hidden.astype(jnp.float32)
    squared = lax.psum(jnp.sum(xf * xf, axis=1), "vocab")
    scale = lax.rsqrt(squared / width + EPS)
    gain_part = lax.dynamic_slice_in_dim(gain, lax.axis_index("vocab") * cols, cols)
    normed = (xf * scale[:, None] * gain_part[None, :]).astype(jnp.bfloat16)
    pieces = lax.all_gather(normed[None], AXES, axis=0, tiled=True)
    groups = pieces.shape[0] // shards
    pieces = pieces.reshape(shards, groups, row_dev, cols)
    weight = head.reshape(shards, cols, vocab_dev)
    raw = jnp.einsum("vgrd,vdc->grc", pieces, weight, preferred_element_type=jnp.float32)
    exps = jnp.exp(CAP * jnp.tanh(raw.reshape(groups * row_dev, vocab_dev) / CAP))
    sums = jnp.sum(exps, axis=1)
    columns = jnp.arange(vocab_dev, dtype=jnp.int32)
    selector = (columns[:, None] == wanted[None, :]).astype(jnp.bfloat16)
    high = lax.reduce_precision(exps, 8, 7)
    low = (exps - high).astype(jnp.bfloat16)
    high = high.astype(jnp.bfloat16)
    picked = jnp.dot(high, selector, preferred_element_type=jnp.float32)
    picked = picked + jnp.dot(low, selector, preferred_element_type=jnp.float32)
    prompt_of = jnp.arange(wanted.shape[0], dtype=jnp.int32) // cands
    terms = jnp.where(row_prompt[:, None] == prompt_of[None, :], picked, 0.0)
    return sums[None, :], terms


def head_kernel(
    sizes, cands, hidden_ref, gain_ref, head_hbm, wanted_ref, prompt_ref, sums_ref, terms_ref,
    gathered, head, selector, mine, theirs,
    head_sem, square_send, square_recv, line_send, pair_send, first_send, second_send, recv,
):
    depth = sizes[2]
    row_dev, cols = hidden_ref.shape
    width, vocab_dev = head.shape
    span = depth * row_dev
    lanes = mine.shape[1]
    core = lax.axis_index("vocab")
    sample = lax.axis_index("sample")
    spot = lax.axis_index("prompt")
    near_x = sample + 1 - 2 * (sample % 2)
    near_y = sample + 2 - 4 * (sample // 2)
    first = near_x * (1 - core) + near_y * core
    second = near_y * (1 - core) + near_x * core
    across = 3 - sample

    pair_at = (1 - core, sample, spot)
    first_at = (core, first, spot)
    second_at = (core, second, spot)

    load = pltpu.make_async_copy(head_hbm, head, head_sem)
    load.start()

    barrier = pltpu.get_barrier_semaphore()
    for step in range(1, depth):
        pl.semaphore_signal(
            barrier, inc=1, device_id=(core, sample, (spot + step) % depth), device_id_type=MESH
        )
    for target in (pair_at, first_at, second_at):
        pl.semaphore_signal(barrier, inc=1, device_id=target, device_id_type=MESH)
    pl.semaphore_wait(barrier, depth + 2)

    def block(half, column, at):
        start = pl.multiple_of((column * depth + at) * row_dev, row_dev)
        return gathered.at[half, pl.ds(start, row_dev)]

    def copy(half, column, at, send_sem, target):
        return pltpu.make_async_remote_copy(
            src_ref=block(half, column, at),
            dst_ref=block(half, column, at),
            send_sem=send_sem,
            recv_sem=recv.at[half, column * depth + at],
            device_id=target,
            device_id_type=MESH,
        )

    def arrived(half, column, at):
        copy(half, column, at, pair_send.at[0], pair_at).wait_recv()

    def to_pair(column, at):
        copy(core, column, at, pair_send.at[column * depth + at], pair_at).start()

    def to_first(at):
        copy(core, sample, at, first_send.at[at], first_at).start()

    def to_second(column, at, turn):
        copy(core, column, at, second_send.at[turn, at], second_at).start()

    xf = hidden_ref[...].astype(jnp.float32)
    squares = xf[:, :lanes] * xf[:, :lanes]
    for begin in range(lanes, cols, lanes):
        squares = squares + xf[:, begin : begin + lanes] * xf[:, begin : begin + lanes]
    mine[...] = squares
    swap = pltpu.make_async_remote_copy(
        src_ref=mine, dst_ref=theirs, send_sem=square_send, recv_sem=square_recv,
        device_id=pair_at, device_id_type=MESH,
    )
    swap.start()
    swap.wait()
    squared = jnp.sum(mine[...] + theirs[...], axis=1, keepdims=True)
    scale = lax.rsqrt(squared / width + EPS)
    own = pl.multiple_of((sample * depth + spot) * row_dev, row_dev)
    gathered[core, pl.ds(own, row_dev), :] = (
        hidden_ref[...].astype(jnp.float32) * scale * gain_ref[core]
    ).astype(jnp.bfloat16)

    to_first(spot)
    to_second(sample, spot, 0)
    for step in range(1, depth):
        at = (spot + step) % depth
        copy(core, sample, spot, line_send.at[step], (core, sample, at)).start()
    to_pair(sample, spot)

    picks = wanted_ref.shape[1]
    rows_of = lax.broadcasted_iota(jnp.int32, (vocab_dev, picks), 0)
    selector[...] = jnp.where(rows_of == wanted_ref[...], 1.0, 0.0).astype(jnp.bfloat16)

    for step in (1, depth - 1, *range(2, depth - 1)):
        at = (spot + step) % depth
        arrived(core, sample, at)
        to_first(at)
        to_second(sample, at, 0)
        to_pair(sample, at)

    def pass_on(column, at):
        arrived(core, column, at)
        to_pair(column, at)

    steps = [(begin, min(begin + 512, vocab_dev)) for begin in range(0, vocab_dev, 512)]
    count = len(steps)
    order = [0, 1, depth - 1, *range(2, depth - 1)]

    def turn(t, carry):
        column = jnp.where(
            t == 0, sample, jnp.where(t == 1, near_x, jnp.where(t == 2, near_y, across))
        )
        start = pl.multiple_of(column * span, span)

        @pl.when(t == 0)
        def _():
            load.wait()
            for step in range(depth):
                arrived(1 - core, sample, (spot + step) % depth)

        @pl.when(t == 1)
        def _():
            for step in order:
                pass_on(second, (spot + step) % depth)
            for step in range(depth):
                arrived(1 - core, first, (spot + step) % depth)
                arrived(1 - core, second, (spot + step) % depth)

        @pl.when(t == 3)
        def _():
            for step in range(depth):
                arrived(1 - core, across, (spot + step) % depth)

        total = jnp.zeros((span, 1), jnp.float32)
        found = None
        for index, (begin, end) in enumerate(steps):
            portion = range(depth * index // count, depth * (index + 1) // count)

            @pl.when(t == 0)
            def _():
                for step in portion:
                    at = (spot + order[step]) % depth
                    arrived(core, first, at)
                    to_second(first, at, 1)
                    to_pair(first, at)

            raw = jnp.dot(
                gathered[0, pl.ds(start, span), :], head[:cols, begin:end],
                preferred_element_type=jnp.float32,
            ) + jnp.dot(
                gathered[1, pl.ds(start, span), :], head[cols:, begin:end],
                preferred_element_type=jnp.float32,
            )
            exps = jnp.exp(CAP * jnp.tanh(raw / CAP))
            total = total + jnp.sum(exps, axis=1, keepdims=True)
            high = exps.astype(jnp.bfloat16)
            low = (exps - high.astype(jnp.float32)).astype(jnp.bfloat16)
            part = jnp.dot(
                high, selector[begin:end, :], preferred_element_type=jnp.float32
            ) + jnp.dot(low, selector[begin:end, :], preferred_element_type=jnp.float32)
            found = part if found is None else found + part

            for step in range(depth):
                if (2 * count * (step + 1) - 1) // depth % count == index:

                    @pl.when(t == 1 + (2 * count * (step + 1) - 1) // depth // count)
                    def _():
                        pass_on(across, (spot + order[step]) % depth)

        prompt_of = lax.broadcasted_iota(jnp.int32, (span, picks), 1) // cands
        terms_ref[pl.ds(start, span), :] = jnp.where(
            prompt_ref[pl.ds(start, span), :] == prompt_of, found, 0.0
        )
        sums_ref[column] = jnp.transpose(jnp.broadcast_to(total, (span, lanes)))[:1, :]
        return carry

    lax.fori_loop(0, 4, turn, 0)

    for step in range(1, depth):
        copy(core, sample, spot, line_send.at[step], pair_at).wait_send()
    for at in range(depth):
        copy(core, sample, at, first_send.at[at], first_at).wait_send()
        copy(core, sample, at, second_send.at[0, at], second_at).wait_send()
        copy(core, first, at, second_send.at[1, at], second_at).wait_send()
        for column in range(sizes[1]):
            copy(core, column, at, pair_send.at[column * depth + at], pair_at).wait_send()


def fused_head(hidden, gain, head, wanted, row_prompt, cands):
    sizes = tuple(lax.axis_size(axis) for axis in AXES)
    row_dev, cols = hidden.shape
    rows, picks = row_prompt.shape[0], wanted.shape[0]
    groups = sizes[1] * sizes[2]
    span = sizes[2] * row_dev
    lanes = 128
    vmem = pl.BlockSpec(memory_space=pltpu.VMEM)
    dma = pltpu.SemaphoreType.DMA
    sums, terms = pl.pallas_call(
        functools.partial(head_kernel, sizes, cands),
        out_shape=(
            jax.ShapeDtypeStruct((sizes[1], 1, span), jnp.float32),
            jax.ShapeDtypeStruct((rows, picks), jnp.float32),
        ),
        in_specs=[vmem, vmem, pl.BlockSpec(memory_space=pl.ANY), vmem, vmem],
        out_specs=(vmem, vmem),
        scratch_shapes=[
            pltpu.VMEM((sizes[0], rows, cols), jnp.bfloat16),
            pltpu.VMEM(head.shape, jnp.bfloat16),
            pltpu.VMEM((head.shape[1], picks), jnp.bfloat16),
            pltpu.VMEM((row_dev, lanes), jnp.float32),
            pltpu.VMEM((row_dev, lanes), jnp.float32),
            dma, dma, dma,
            dma((sizes[2],)),
            dma((groups,)),
            dma((sizes[2],)),
            dma((2, sizes[2])),
            dma((sizes[0], groups)),
        ],
        compiler_params=pltpu.CompilerParams(
            collective_id=0, has_side_effects=True, vmem_limit_bytes=54 << 20
        ),
    )(hidden, gain.reshape(sizes[0], 1, cols), head, wanted[None, :], row_prompt[:, None])
    return sums.reshape(1, rows), terms


def body(hidden, gain, head, candidates, row_prompt):
    row_dev = hidden.shape[0]
    prompts, cands = candidates.shape
    offset = lax.axis_index(AXES) * head.shape[1]
    wanted = candidates.reshape(prompts * cands) - offset
    corners = lax.axis_size("vocab") == 2 and lax.axis_size("sample") == 4
    local = fused_head if corners else plain_head
    sums, terms = local(hidden, gain, head, wanted, row_prompt, cands)
    votes, totals = finish(sums, terms)
    group = lax.axis_index(("sample", "prompt"))
    row_lse = lax.dynamic_slice_in_dim(jnp.log(totals[0]), group * row_dev, row_dev, 0)
    return votes.reshape(prompts, cands), row_lse


def solution(mesh):
    placed = (
        P(("sample", "prompt"), "vocab"),
        P(),
        P(None, AXES),
        P(),
        P(),
    )
    return jax.shard_map(
        body, mesh=mesh, in_specs=placed, out_specs=(P(), P(("sample", "prompt"))), check_vma=False
    )
```

```python
import functools

import jax
import jax.numpy as jnp
from jax import lax
from jax.experimental import pallas as pl
from jax.experimental.pallas import tpu as pltpu
from jax.sharding import PartitionSpec as P

CAP = 30.0
EPS = 1e-06
AXES = ("vocab", "sample", "prompt")
MESH = pl.DeviceIdType.MESH


def place(flat, sizes):
    return (flat // (sizes[1] * sizes[2]), flat // sizes[2] % sizes[1], flat % sizes[2])


def finish_kernel(
    sizes, sums_ref, terms_ref, tally_ref, totals_ref,
    sums_in, part, part_in, send_a, recv_a, send_b, recv_b,
):
    devices = sizes[0] * sizes[1] * sizes[2]
    me = lax.axis_index(AXES)
    barrier = pltpu.get_barrier_semaphore()

    def greet(step, carry):
        peer = (me + step) % devices
        pl.semaphore_signal(barrier, inc=1, device_id=place(peer, sizes), device_id_type=MESH)
        return carry

    lax.fori_loop(1, devices, greet, 0)
    pl.semaphore_wait(barrier, devices - 1)

    def push(source, target, send_sem, recv_sem):
        def out(step, carry):
            peer = (me + step) % devices
            pltpu.make_async_remote_copy(
                src_ref=source,
                dst_ref=target.at[me],
                send_sem=send_sem.at[step],
                recv_sem=recv_sem.at[me],
                device_id=place(peer, sizes),
                device_id_type=MESH,
            ).start()
            return carry

        lax.fori_loop(1, devices, out, 0)

    def collect(source, target, send_sem, recv_sem):
        def arrive(step, carry):
            peer = (me + step) % devices
            pltpu.make_async_remote_copy(
                src_ref=source,
                dst_ref=target.at[peer],
                send_sem=send_sem.at[step],
                recv_sem=recv_sem.at[peer],
                device_id=place(peer, sizes),
                device_id_type=MESH,
            ).wait()
            return carry

        lax.fori_loop(1, devices, arrive, 0)

    push(sums_ref, sums_in, send_a, recv_a)
    sums_in[me] = sums_ref[...]
    collect(sums_ref, sums_in, send_a, recv_a)
    total = jnp.sum(sums_in[...], axis=0)
    totals_ref[...] = total
    part[...] = lax.dot_general(
        1.0 / total, terms_ref[...], (((1,), (1,)), ((), ())),
        precision=lax.Precision.HIGHEST, preferred_element_type=jnp.float32,
    )
    push(part, part_in, send_b, recv_b)
    part_in[me] = part[...]
    collect(part, part_in, send_b, recv_b)
    tally_ref[...] = jnp.log(jnp.sum(part_in[...], axis=0))


def finish(sums, terms):
    sizes = tuple(lax.axis_size(axis) for axis in AXES)
    devices = sizes[0] * sizes[1] * sizes[2]
    picks, rows = terms.shape
    vmem = pl.BlockSpec(memory_space=pltpu.VMEM)
    return pl.pallas_call(
        functools.partial(finish_kernel, sizes),
        out_shape=(
            jax.ShapeDtypeStruct((1, picks), jnp.float32),
            jax.ShapeDtypeStruct((1, rows), jnp.float32),
        ),
        in_specs=[vmem] * 2,
        out_specs=(vmem, vmem),
        scratch_shapes=[
            pltpu.VMEM((devices, 1, rows), jnp.float32),
            pltpu.VMEM((1, picks), jnp.float32),
            pltpu.VMEM((devices, 1, picks), jnp.float32),
            pltpu.SemaphoreType.DMA((devices,)),
            pltpu.SemaphoreType.DMA((devices,)),
            pltpu.SemaphoreType.DMA((devices,)),
            pltpu.SemaphoreType.DMA((devices,)),
        ],
        compiler_params=pltpu.CompilerParams(
            collective_id=1, has_side_effects=True, vmem_limit_bytes=24 << 20
        ),
    )(sums, terms)


def plain_head(hidden, gain, head, wanted, row_prompt, cands):
    width = head.shape[0]
    vocab_dev = head.shape[1]
    shards = lax.axis_size("vocab")
    row_dev = hidden.shape[0]
    cols = hidden.shape[1]
    xf = hidden.astype(jnp.float32)
    squared = lax.psum(jnp.sum(xf * xf, axis=1), "vocab")
    scale = lax.rsqrt(squared / width + EPS)
    gain_part = lax.dynamic_slice_in_dim(gain, lax.axis_index("vocab") * cols, cols)
    normed = (xf * scale[:, None] * gain_part[None, :]).astype(jnp.bfloat16)
    pieces = lax.all_gather(normed[None], AXES, axis=0, tiled=True)
    groups = pieces.shape[0] // shards
    pieces = pieces.reshape(shards, groups, row_dev, cols)
    weight = head.reshape(shards, cols, vocab_dev)
    raw = jnp.einsum("vgrd,vdc->grc", pieces, weight, preferred_element_type=jnp.float32)
    exps = jnp.exp(CAP * jnp.tanh(raw.reshape(groups * row_dev, vocab_dev) / CAP))
    sums = jnp.sum(exps, axis=1)
    columns = jnp.arange(vocab_dev, dtype=jnp.int32)
    selector = (columns[:, None] == wanted[None, :]).astype(jnp.bfloat16)
    high = lax.reduce_precision(exps, 8, 7)
    low = (exps - high).astype(jnp.bfloat16)
    high = high.astype(jnp.bfloat16)
    picked = jnp.dot(high, selector, preferred_element_type=jnp.float32)
    picked = picked + jnp.dot(low, selector, preferred_element_type=jnp.float32)
    prompt_of = jnp.arange(wanted.shape[0], dtype=jnp.int32) // cands
    terms = jnp.where(row_prompt[:, None] == prompt_of[None, :], picked, 0.0)
    return sums[None, :], terms.T


def head_kernel(
    sizes, cands, hidden_ref, gain_ref, head_hbm, wanted_ref, prompt_ref, sums_ref, terms_ref,
    gathered, head, selector, mine, theirs,
    head_sem, square_send, square_recv, line_send, pair_send, first_send, second_send, recv,
):
    depth = sizes[2]
    row_dev, cols = hidden_ref.shape
    vocab_dev, width = head.shape
    span = depth * row_dev
    lanes = mine.shape[1]
    core = lax.axis_index("vocab")
    sample = lax.axis_index("sample")
    spot = lax.axis_index("prompt")
    near_x = sample + 1 - 2 * (sample % 2)
    near_y = sample + 2 - 4 * (sample // 2)
    first = near_x * (1 - core) + near_y * core
    second = near_y * (1 - core) + near_x * core
    across = 3 - sample

    pair_at = (1 - core, sample, spot)
    first_at = (core, first, spot)
    second_at = (core, second, spot)

    load = pltpu.make_async_copy(head_hbm, head, head_sem)
    load.start()

    barrier = pltpu.get_barrier_semaphore()
    for step in range(1, depth):
        pl.semaphore_signal(
            barrier, inc=1, device_id=(core, sample, (spot + step) % depth), device_id_type=MESH
        )
    for target in (pair_at, first_at, second_at):
        pl.semaphore_signal(barrier, inc=1, device_id=target, device_id_type=MESH)
    pl.semaphore_wait(barrier, depth + 2)

    def block(half, column, at):
        start = pl.multiple_of((column * depth + at) * row_dev, row_dev)
        return gathered.at[half, pl.ds(start, row_dev)]

    def copy(half, column, at, send_sem, target):
        return pltpu.make_async_remote_copy(
            src_ref=block(half, column, at),
            dst_ref=block(half, column, at),
            send_sem=send_sem,
            recv_sem=recv.at[half, column * depth + at],
            device_id=target,
            device_id_type=MESH,
        )

    def arrived(half, column, at):
        copy(half, column, at, pair_send.at[0], pair_at).wait_recv()

    def to_pair(column, at):
        copy(core, column, at, pair_send.at[column * depth + at], pair_at).start()

    def to_first(at):
        copy(core, sample, at, first_send.at[at], first_at).start()

    def to_second(column, at, turn):
        copy(core, column, at, second_send.at[turn, at], second_at).start()

    xf = hidden_ref[...].astype(jnp.float32)
    squares = xf[:, :lanes] * xf[:, :lanes]
    for begin in range(lanes, cols, lanes):
        squares = squares + xf[:, begin : begin + lanes] * xf[:, begin : begin + lanes]
    mine[...] = squares
    swap = pltpu.make_async_remote_copy(
        src_ref=mine, dst_ref=theirs, send_sem=square_send, recv_sem=square_recv,
        device_id=pair_at, device_id_type=MESH,
    )
    swap.start()
    swap.wait()
    squared = jnp.sum(mine[...] + theirs[...], axis=1, keepdims=True)
    scale = lax.rsqrt(squared / width + EPS)
    own = pl.multiple_of((sample * depth + spot) * row_dev, row_dev)
    gathered[core, pl.ds(own, row_dev), :] = (
        hidden_ref[...].astype(jnp.float32) * scale * gain_ref[core]
    ).astype(jnp.bfloat16)

    to_first(spot)
    to_second(sample, spot, 0)
    for step in range(1, depth):
        at = (spot + step) % depth
        copy(core, sample, spot, line_send.at[step], (core, sample, at)).start()
    to_pair(sample, spot)

    picks = wanted_ref.shape[0]
    columns_of = lax.broadcasted_iota(jnp.int32, (picks, vocab_dev), 1)
    selector[...] = jnp.where(columns_of == wanted_ref[...], 1.0, 0.0).astype(jnp.bfloat16)

    for step in (1, depth - 1, *range(2, depth - 1)):
        at = (spot + step) % depth
        arrived(core, sample, at)
        to_first(at)
        to_second(sample, at, 0)
        to_pair(sample, at)

    def pass_on(column, at):
        arrived(core, column, at)
        to_pair(column, at)

    steps = [(begin, min(begin + 512, vocab_dev)) for begin in range(0, vocab_dev, 512)]
    count = len(steps)
    order = [0, 1, depth - 1, *range(2, depth - 1)]

    def turn(t, carry):
        column = jnp.where(
            t == 0, sample, jnp.where(t == 1, near_x, jnp.where(t == 2, near_y, across))
        )
        start = pl.multiple_of(column * span, span)

        @pl.when(t == 0)
        def _():
            load.wait()
            for step in range(depth):
                arrived(1 - core, sample, (spot + step) % depth)

        @pl.when(t == 1)
        def _():
            for step in order:
                pass_on(second, (spot + step) % depth)
            for step in range(depth):
                arrived(1 - core, first, (spot + step) % depth)
                arrived(1 - core, second, (spot + step) % depth)

        @pl.when(t == 3)
        def _():
            for step in range(depth):
                arrived(1 - core, across, (spot + step) % depth)

        total = jnp.zeros((span, 1), jnp.float32)
        found = None
        for index, (begin, end) in enumerate(steps):
            portion = range(depth * index // count, depth * (index + 1) // count)

            @pl.when(t == 0)
            def _():
                for step in portion:
                    at = (spot + order[step]) % depth
                    arrived(core, first, at)
                    to_second(first, at, 1)
                    to_pair(first, at)

            raw = lax.dot_general(
                gathered[0, pl.ds(start, span), :], head[begin:end, :cols],
                (((1,), (1,)), ((), ())), preferred_element_type=jnp.float32,
            ) + lax.dot_general(
                gathered[1, pl.ds(start, span), :], head[begin:end, cols:],
                (((1,), (1,)), ((), ())), preferred_element_type=jnp.float32,
            )
            exps = jnp.exp(CAP * jnp.tanh(raw / CAP))
            total = total + jnp.sum(exps, axis=1, keepdims=True)
            high = exps.astype(jnp.bfloat16)
            low = (exps - high.astype(jnp.float32)).astype(jnp.bfloat16)
            part = lax.dot_general(
                selector[:, begin:end], high,
                (((1,), (1,)), ((), ())), preferred_element_type=jnp.float32,
            ) + lax.dot_general(
                selector[:, begin:end], low,
                (((1,), (1,)), ((), ())), preferred_element_type=jnp.float32,
            )
            found = part if found is None else found + part

            for step in range(depth):
                if (2 * count * (step + 1) - 1) // depth % count == index:

                    @pl.when(t == 1 + (2 * count * (step + 1) - 1) // depth // count)
                    def _():
                        pass_on(across, (spot + order[step]) % depth)

        prompt_of = lax.broadcasted_iota(jnp.int32, (picks, span), 0) // cands
        terms_ref[:, pl.ds(start, span)] = jnp.where(
            prompt_ref[:, pl.ds(start, span)] == prompt_of, found, 0.0
        )
        sums_ref[column] = jnp.transpose(jnp.broadcast_to(total, (span, lanes)))[:1, :]
        return carry

    lax.fori_loop(0, 4, turn, 0)

    for step in range(1, depth):
        copy(core, sample, spot, line_send.at[step], pair_at).wait_send()
    for at in range(depth):
        copy(core, sample, at, first_send.at[at], first_at).wait_send()
        copy(core, sample, at, second_send.at[0, at], second_at).wait_send()
        copy(core, first, at, second_send.at[1, at], second_at).wait_send()
        for column in range(sizes[1]):
            copy(core, column, at, pair_send.at[column * depth + at], pair_at).wait_send()


def fused_head(hidden, gain, head, wanted, row_prompt, cands):
    sizes = tuple(lax.axis_size(axis) for axis in AXES)
    row_dev, cols = hidden.shape
    rows, picks = row_prompt.shape[0], wanted.shape[0]
    groups = sizes[1] * sizes[2]
    span = sizes[2] * row_dev
    lanes = 128
    vmem = pl.BlockSpec(memory_space=pltpu.VMEM)
    dma = pltpu.SemaphoreType.DMA
    sums, terms = pl.pallas_call(
        functools.partial(head_kernel, sizes, cands),
        out_shape=(
            jax.ShapeDtypeStruct((sizes[1], 1, span), jnp.float32),
            jax.ShapeDtypeStruct((picks, rows), jnp.float32),
        ),
        in_specs=[vmem, vmem, pl.BlockSpec(memory_space=pl.ANY), vmem, vmem],
        out_specs=(vmem, vmem),
        scratch_shapes=[
            pltpu.VMEM((sizes[0], rows, cols), jnp.bfloat16),
            pltpu.VMEM(head.shape[::-1], jnp.bfloat16),
            pltpu.VMEM((picks, head.shape[1]), jnp.bfloat16),
            pltpu.VMEM((row_dev, lanes), jnp.float32),
            pltpu.VMEM((row_dev, lanes), jnp.float32),
            dma, dma, dma,
            dma((sizes[2],)),
            dma((groups,)),
            dma((sizes[2],)),
            dma((2, sizes[2])),
            dma((sizes[0], groups)),
        ],
        compiler_params=pltpu.CompilerParams(
            collective_id=0, has_side_effects=True, vmem_limit_bytes=54 << 20
        ),
    )(hidden, gain.reshape(sizes[0], 1, cols), head.T, wanted[:, None], row_prompt[None, :])
    return sums.reshape(1, rows), terms


def body(hidden, gain, head, candidates, row_prompt):
    row_dev = hidden.shape[0]
    prompts, cands = candidates.shape
    offset = lax.axis_index(AXES) * head.shape[1]
    wanted = candidates.reshape(prompts * cands) - offset
    corners = lax.axis_size("vocab") == 2 and lax.axis_size("sample") == 4
    local = fused_head if corners else plain_head
    sums, terms = local(hidden, gain, head, wanted, row_prompt, cands)
    votes, totals = finish(sums, terms)
    group = lax.axis_index(("sample", "prompt"))
    row_lse = lax.dynamic_slice_in_dim(jnp.log(totals[0]), group * row_dev, row_dev, 0)
    return votes.reshape(prompts, cands), row_lse


def solution(mesh):
    placed = (
        P(("sample", "prompt"), "vocab"),
        P(),
        P(None, AXES),
        P(),
        P(),
    )
    return jax.shard_map(
        body, mesh=mesh, in_specs=placed, out_specs=(P(), P(("sample", "prompt"))), check_vma=False
    )
```

```python
import functools

import jax
import jax.numpy as jnp
from jax import lax
from jax.experimental import pallas as pl
from jax.experimental.pallas import tpu as pltpu
from jax.sharding import PartitionSpec as P

CAP = 30.0
EPS = 1e-06
AXES = ("vocab", "sample", "prompt")
MESH = pl.DeviceIdType.MESH


def place(flat, sizes):
    return (flat // (sizes[1] * sizes[2]), flat // sizes[2] % sizes[1], flat % sizes[2])


def finish_kernel(
    sizes, sums_ref, terms_ref, tally_ref, totals_ref,
    sums_in, part, part_in, send_a, recv_a, send_b, recv_b,
):
    devices = sizes[0] * sizes[1] * sizes[2]
    me = lax.axis_index(AXES)
    barrier = pltpu.get_barrier_semaphore()

    def greet(step, carry):
        peer = (me + step) % devices
        pl.semaphore_signal(barrier, inc=1, device_id=place(peer, sizes), device_id_type=MESH)
        return carry

    lax.fori_loop(1, devices, greet, 0)
    pl.semaphore_wait(barrier, devices - 1)

    def push(source, target, send_sem, recv_sem):
        def out(step, carry):
            peer = (me + step) % devices
            pltpu.make_async_remote_copy(
                src_ref=source,
                dst_ref=target.at[me],
                send_sem=send_sem.at[step],
                recv_sem=recv_sem.at[me],
                device_id=place(peer, sizes),
                device_id_type=MESH,
            ).start()
            return carry

        lax.fori_loop(1, devices, out, 0)

    def collect(source, target, send_sem, recv_sem):
        def arrive(step, carry):
            peer = (me + step) % devices
            pltpu.make_async_remote_copy(
                src_ref=source,
                dst_ref=target.at[peer],
                send_sem=send_sem.at[step],
                recv_sem=recv_sem.at[peer],
                device_id=place(peer, sizes),
                device_id_type=MESH,
            ).wait()
            return carry

        lax.fori_loop(1, devices, arrive, 0)

    push(sums_ref, sums_in, send_a, recv_a)
    sums_in[me] = sums_ref[...]
    collect(sums_ref, sums_in, send_a, recv_a)
    total = jnp.sum(sums_in[...], axis=0)
    totals_ref[...] = total
    part[...] = lax.dot_general(
        1.0 / total, terms_ref[...], (((1,), (1,)), ((), ())),
        precision=lax.Precision.HIGHEST, preferred_element_type=jnp.float32,
    )
    push(part, part_in, send_b, recv_b)
    part_in[me] = part[...]
    collect(part, part_in, send_b, recv_b)
    tally_ref[...] = jnp.log(jnp.sum(part_in[...], axis=0))


def finish(sums, terms):
    sizes = tuple(lax.axis_size(axis) for axis in AXES)
    devices = sizes[0] * sizes[1] * sizes[2]
    picks, rows = terms.shape
    vmem = pl.BlockSpec(memory_space=pltpu.VMEM)
    return pl.pallas_call(
        functools.partial(finish_kernel, sizes),
        out_shape=(
            jax.ShapeDtypeStruct((1, picks), jnp.float32),
            jax.ShapeDtypeStruct((1, rows), jnp.float32),
        ),
        in_specs=[vmem] * 2,
        out_specs=(vmem, vmem),
        scratch_shapes=[
            pltpu.VMEM((devices, 1, rows), jnp.float32),
            pltpu.VMEM((1, picks), jnp.float32),
            pltpu.VMEM((devices, 1, picks), jnp.float32),
            pltpu.SemaphoreType.DMA((devices,)),
            pltpu.SemaphoreType.DMA((devices,)),
            pltpu.SemaphoreType.DMA((devices,)),
            pltpu.SemaphoreType.DMA((devices,)),
        ],
        compiler_params=pltpu.CompilerParams(
            collective_id=1, has_side_effects=True, vmem_limit_bytes=24 << 20
        ),
    )(sums, terms)


def plain_head(hidden, gain, head, wanted, row_prompt, cands):
    width = head.shape[0]
    vocab_dev = head.shape[1]
    shards = lax.axis_size("vocab")
    row_dev = hidden.shape[0]
    cols = hidden.shape[1]
    xf = hidden.astype(jnp.float32)
    squared = lax.psum(jnp.sum(xf * xf, axis=1), "vocab")
    scale = lax.rsqrt(squared / width + EPS)
    gain_part = lax.dynamic_slice_in_dim(gain, lax.axis_index("vocab") * cols, cols)
    normed = (xf * scale[:, None] * gain_part[None, :]).astype(jnp.bfloat16)
    pieces = lax.all_gather(normed[None], AXES, axis=0, tiled=True)
    groups = pieces.shape[0] // shards
    pieces = pieces.reshape(shards, groups, row_dev, cols)
    weight = head.reshape(shards, cols, vocab_dev)
    raw = jnp.einsum("vgrd,vdc->grc", pieces, weight, preferred_element_type=jnp.float32)
    exps = jnp.exp(CAP * jnp.tanh(raw.reshape(groups * row_dev, vocab_dev) / CAP))
    sums = jnp.sum(exps, axis=1)
    columns = jnp.arange(vocab_dev, dtype=jnp.int32)
    selector = (columns[:, None] == wanted[None, :]).astype(jnp.bfloat16)
    high = lax.reduce_precision(exps, 8, 7)
    low = (exps - high).astype(jnp.bfloat16)
    high = high.astype(jnp.bfloat16)
    picked = jnp.dot(high, selector, preferred_element_type=jnp.float32)
    picked = picked + jnp.dot(low, selector, preferred_element_type=jnp.float32)
    prompt_of = jnp.arange(wanted.shape[0], dtype=jnp.int32) // cands
    terms = jnp.where(row_prompt[:, None] == prompt_of[None, :], picked, 0.0)
    return sums[None, :], terms.T


def head_kernel(
    sizes, cands, hidden_ref, gain_ref, head_hbm, wanted_ref, prompt_ref, sums_ref, terms_ref,
    gathered, head, selector, mine, theirs,
    head_sem, square_send, square_recv, line_send, pair_send, first_send, second_send, recv,
):
    depth = sizes[2]
    row_dev, cols = hidden_ref.shape
    vocab_dev, width = head.shape
    span = depth * row_dev
    lanes = mine.shape[1]
    core = lax.axis_index("vocab")
    sample = lax.axis_index("sample")
    spot = lax.axis_index("prompt")
    near_x = sample + 1 - 2 * (sample % 2)
    near_y = sample + 2 - 4 * (sample // 2)
    first = near_x * (1 - core) + near_y * core
    second = near_y * (1 - core) + near_x * core
    across = 3 - sample

    pair_at = (1 - core, sample, spot)
    first_at = (core, first, spot)
    second_at = (core, second, spot)

    load = pltpu.make_async_copy(head_hbm, head, head_sem)
    load.start()

    barrier = pltpu.get_barrier_semaphore()
    for step in range(1, depth):
        pl.semaphore_signal(
            barrier, inc=1, device_id=(core, sample, (spot + step) % depth), device_id_type=MESH
        )
    for target in (pair_at, first_at, second_at):
        pl.semaphore_signal(barrier, inc=1, device_id=target, device_id_type=MESH)
    pl.semaphore_wait(barrier, depth + 2)

    def block(half, column, at):
        start = pl.multiple_of((column * depth + at) * row_dev, row_dev)
        return gathered.at[half, pl.ds(start, row_dev)]

    def copy(half, column, at, send_sem, target):
        return pltpu.make_async_remote_copy(
            src_ref=block(half, column, at),
            dst_ref=block(half, column, at),
            send_sem=send_sem,
            recv_sem=recv.at[half, column * depth + at],
            device_id=target,
            device_id_type=MESH,
        )

    def arrived(half, column, at):
        copy(half, column, at, pair_send.at[0], pair_at).wait_recv()

    def to_pair(column, at):
        copy(core, column, at, pair_send.at[column * depth + at], pair_at).start()

    def to_first(at):
        copy(core, sample, at, first_send.at[at], first_at).start()

    def to_second(column, at, turn):
        copy(core, column, at, second_send.at[turn, at], second_at).start()

    xf = hidden_ref[...].astype(jnp.float32)
    squares = xf[:, :lanes] * xf[:, :lanes]
    for begin in range(lanes, cols, lanes):
        squares = squares + xf[:, begin : begin + lanes] * xf[:, begin : begin + lanes]
    mine[...] = squares
    swap = pltpu.make_async_remote_copy(
        src_ref=mine, dst_ref=theirs, send_sem=square_send, recv_sem=square_recv,
        device_id=pair_at, device_id_type=MESH,
    )
    swap.start()
    swap.wait()
    squared = jnp.sum(mine[...] + theirs[...], axis=1, keepdims=True)
    scale = lax.rsqrt(squared / width + EPS)
    own = pl.multiple_of((sample * depth + spot) * row_dev, row_dev)
    gathered[core, pl.ds(own, row_dev), :] = (
        hidden_ref[...].astype(jnp.float32) * scale * gain_ref[core]
    ).astype(jnp.bfloat16)

    to_first(spot)
    to_second(sample, spot, 0)
    for step in range(1, depth):
        at = (spot + step) % depth
        copy(core, sample, spot, line_send.at[step], (core, sample, at)).start()
    to_pair(sample, spot)

    picks = wanted_ref.shape[0]
    columns_of = lax.broadcasted_iota(jnp.int32, (picks, vocab_dev), 1)
    selector[...] = jnp.where(columns_of == wanted_ref[...], 1.0, 0.0).astype(jnp.bfloat16)

    for step in (1, depth - 1, *range(2, depth - 1)):
        at = (spot + step) % depth
        arrived(core, sample, at)
        to_first(at)
        to_second(sample, at, 0)
        to_pair(sample, at)

    def pass_on(column, at):
        arrived(core, column, at)
        to_pair(column, at)

    steps = [(begin, min(begin + 512, vocab_dev)) for begin in range(0, vocab_dev, 512)]
    count = len(steps)
    order = [0, 1, depth - 1, *range(2, depth - 1)]

    def turn(t, carry):
        column = jnp.where(
            t == 0, sample, jnp.where(t == 1, near_x, jnp.where(t == 2, near_y, across))
        )
        start = pl.multiple_of(column * span, span)

        @pl.when(t == 0)
        def _():
            load.wait()
            for step in range(depth):
                arrived(1 - core, sample, (spot + step) % depth)

        @pl.when(t == 1)
        def _():
            for step in range(depth):
                arrived(1 - core, first, (spot + step) % depth)
                arrived(1 - core, second, (spot + step) % depth)

        @pl.when(t == 3)
        def _():
            for step in range(depth):
                arrived(1 - core, across, (spot + step) % depth)

        total = jnp.zeros((span, 1), jnp.float32)
        found = None
        for index, (begin, end) in enumerate(steps):
            portion = range(depth * index // count, depth * (index + 1) // count)

            @pl.when(t == 0)
            def _():
                for step in portion:
                    at = (spot + order[step]) % depth
                    arrived(core, first, at)
                    to_second(first, at, 1)
                    to_pair(first, at)
                    pass_on(second, at)

            raw = lax.dot_general(
                gathered[0, pl.ds(start, span), :], head[begin:end, :cols],
                (((1,), (1,)), ((), ())), preferred_element_type=jnp.float32,
            ) + lax.dot_general(
                gathered[1, pl.ds(start, span), :], head[begin:end, cols:],
                (((1,), (1,)), ((), ())), preferred_element_type=jnp.float32,
            )
            exps = jnp.exp(CAP * jnp.tanh(raw / CAP))
            total = total + jnp.sum(exps, axis=1, keepdims=True)
            high = exps.astype(jnp.bfloat16)
            low = (exps - high.astype(jnp.float32)).astype(jnp.bfloat16)
            part = lax.dot_general(
                selector[:, begin:end], high,
                (((1,), (1,)), ((), ())), preferred_element_type=jnp.float32,
            ) + lax.dot_general(
                selector[:, begin:end], low,
                (((1,), (1,)), ((), ())), preferred_element_type=jnp.float32,
            )
            found = part if found is None else found + part

            for step in range(depth):
                if (2 * count * (step + 1) - 1) // depth % count == index:

                    @pl.when(t == 1 + (2 * count * (step + 1) - 1) // depth // count)
                    def _():
                        pass_on(across, (spot + order[step]) % depth)

        prompt_of = lax.broadcasted_iota(jnp.int32, (picks, span), 0) // cands
        terms_ref[:, pl.ds(start, span)] = jnp.where(
            prompt_ref[:, pl.ds(start, span)] == prompt_of, found, 0.0
        )
        sums_ref[column] = jnp.transpose(jnp.broadcast_to(total, (span, lanes)))[:1, :]
        return carry

    lax.fori_loop(0, 4, turn, 0)

    for step in range(1, depth):
        copy(core, sample, spot, line_send.at[step], pair_at).wait_send()
    for at in range(depth):
        copy(core, sample, at, first_send.at[at], first_at).wait_send()
        copy(core, sample, at, second_send.at[0, at], second_at).wait_send()
        copy(core, first, at, second_send.at[1, at], second_at).wait_send()
        for column in range(sizes[1]):
            copy(core, column, at, pair_send.at[column * depth + at], pair_at).wait_send()


def fused_head(hidden, gain, head, wanted, row_prompt, cands):
    sizes = tuple(lax.axis_size(axis) for axis in AXES)
    row_dev, cols = hidden.shape
    rows, picks = row_prompt.shape[0], wanted.shape[0]
    groups = sizes[1] * sizes[2]
    span = sizes[2] * row_dev
    lanes = 128
    vmem = pl.BlockSpec(memory_space=pltpu.VMEM)
    dma = pltpu.SemaphoreType.DMA
    sums, terms = pl.pallas_call(
        functools.partial(head_kernel, sizes, cands),
        out_shape=(
            jax.ShapeDtypeStruct((sizes[1], 1, span), jnp.float32),
            jax.ShapeDtypeStruct((picks, rows), jnp.float32),
        ),
        in_specs=[vmem, vmem, pl.BlockSpec(memory_space=pl.ANY), vmem, vmem],
        out_specs=(vmem, vmem),
        scratch_shapes=[
            pltpu.VMEM((sizes[0], rows, cols), jnp.bfloat16),
            pltpu.VMEM(head.shape[::-1], jnp.bfloat16),
            pltpu.VMEM((picks, head.shape[1]), jnp.bfloat16),
            pltpu.VMEM((row_dev, lanes), jnp.float32),
            pltpu.VMEM((row_dev, lanes), jnp.float32),
            dma, dma, dma,
            dma((sizes[2],)),
            dma((groups,)),
            dma((sizes[2],)),
            dma((2, sizes[2])),
            dma((sizes[0], groups)),
        ],
        compiler_params=pltpu.CompilerParams(
            collective_id=0, has_side_effects=True, vmem_limit_bytes=54 << 20
        ),
    )(hidden, gain.reshape(sizes[0], 1, cols), head.T, wanted[:, None], row_prompt[None, :])
    return sums.reshape(1, rows), terms


def body(hidden, gain, head, candidates, row_prompt):
    row_dev = hidden.shape[0]
    prompts, cands = candidates.shape
    offset = lax.axis_index(AXES) * head.shape[1]
    wanted = candidates.reshape(prompts * cands) - offset
    corners = lax.axis_size("vocab") == 2 and lax.axis_size("sample") == 4
    local = fused_head if corners else plain_head
    sums, terms = local(hidden, gain, head, wanted, row_prompt, cands)
    votes, totals = finish(sums, terms)
    group = lax.axis_index(("sample", "prompt"))
    row_lse = lax.dynamic_slice_in_dim(jnp.log(totals[0]), group * row_dev, row_dev, 0)
    return votes.reshape(prompts, cands), row_lse


def solution(mesh):
    placed = (
        P(("sample", "prompt"), "vocab"),
        P(),
        P(None, AXES),
        P(),
        P(),
    )
    return jax.shard_map(
        body, mesh=mesh, in_specs=placed, out_specs=(P(), P(("sample", "prompt"))), check_vma=False
    )
```
